32 devices in a mesh: pipe: 8 (over z, x), tensor: 4 (over y, core).
Axes of the slice: x: 2, y: 2, z: 4, core: 2. Of those that a mesh axis runs over, the one named last changes fastest.
Arguments:
- x_saved: bfloat16 [8, 2, 4096, 128], P('pipe', None, 'tensor'), may hold values from -6 to 6
- seed_grad: bfloat16 [8, 2, 4096, 128], P('pipe', None, 'tensor'), may hold values from -6 to 6
- gate_blocks: bfloat16 [8, 4, 7, 20, 4096], P('pipe', 'tensor'), may hold values from -0.1875 to 0.1875
- up_blocks: bfloat16 [8, 4, 7, 20, 4096], P('pipe', 'tensor'), may hold values from -0.1875 to 0.1875
- down_blocks: bfloat16 [8, 4, 7, 20, 4096], P('pipe', 'tensor'), may hold values from -0.1875 to 0.1875
- gate_rows: int32 [8, 4, 7, 20], P('pipe', 'tensor'), may hold values from -1 to 63, as said below
- down_rows: int32 [8, 4, 7, 20], P('pipe', 'tensor'), may hold values from -1 to 63, as said below
Outputs:
- grad_input: bfloat16 [8, 2, 4096, 128], P('pipe', None, 'tensor')
The draws below stay inside these ranges and needn't reach their ends.
Inputs may be any that keep to these rules, and one draw needn't show every extreme that they name: `gate_rows`: in one column of tiles the non-negative entries are distinct and come before the -1 entries. All columns of one tensor shard of one section hold the same number of kept tiles, from 12 to 20, and in every section one shard holds 20 in every column. `down_rows`: as for gate_rows, drawn independently.
All inputs are finite; a program needn't handle non-finite values.
Results may differ from the reference program's by a relative error of at most 0.007.
Values may be sent and summed in bfloat16 or wider, within the bound.
A program may use at most 128 MiB of HBM per device.

```python
import jax
import jax.numpy as jnp
from jax import lax

D = 4096
BLK = 64
RCAP = 20
TOK = 128
MB = 2
RB = 64
COLS = 14
RLOW = 12
N_PIPE = 8
N_TENSOR = 4


def block_rows(key):
    sections = N_PIPE // 2
    slot_total = sections * N_TENSOR * COLS
    key_list = jax.random.split(key, slot_total + 2)
    orders = jax.vmap(lambda one_key: jax.random.permutation(one_key, RB))(key_list[:slot_total])[:, :RCAP]
    orders = orders.reshape(sections, N_TENSOR, COLS, RCAP)
    fill_counts = jax.random.randint(key_list[slot_total], (sections, N_TENSOR), RLOW, RCAP + 1)
    busiest = jax.random.randint(key_list[slot_total + 1], (sections,), 0, N_TENSOR)
    fill_counts = jnp.where(jnp.arange(N_TENSOR)[None, :] == busiest[:, None], RCAP, fill_counts)
    slot_index = jnp.arange(RCAP)
    row_table = jnp.where(slot_index[None, None, None, :] < fill_counts[:, :, None, None], orders, -1)
    row_table = row_table.reshape(sections, N_TENSOR, 2, COLS // 2, RCAP).transpose(0, 2, 1, 3, 4)
    return row_table.reshape(N_PIPE, N_TENSOR, COLS // 2, RCAP).astype(jnp.int32)


def draw_gate_rows(key, part):
    return block_rows(jax.random.fold_in(key, 11))


def draw_down_rows(key, part):
    return block_rows(jax.random.fold_in(key, 23))


def levels(rng, extent, shards, low, top_value):
    def one(axis_at, parts):
        heights = jax.random.uniform(jax.random.fold_in(jax.random.fold_in(rng, 6), axis_at), (parts,), jnp.float32, low / len(shards), top_value / len(shards))
        return jnp.repeat(jnp.exp(heights), extent[axis_at] // parts).reshape((-1,) + (1,) * (len(extent) - axis_at - 1))

    level = one(*shards[0])
    for cut in shards[1:]:
        level = level * one(*cut)
    return level


def noise(key, dims, deviation, bound, shards=(), kind=jnp.bfloat16):
    gain = levels(key, dims, shards, -0.22, 0.18) if shards else 1.0
    drawn = jax.random.normal(key, dims, jnp.float32) * deviation * gain
    return jnp.minimum(jnp.maximum(drawn, -bound), bound).astype(kind)


def setup_inputs(seed: int = 0) -> dict:
    arg_keys = jax.random.split(jax.random.key(seed), 8)
    x_saved = noise(arg_keys[0], (N_PIPE, MB, D, TOK), 1.0, 6.0, ((0, 8), (2, 4)))
    seed_grad = noise(arg_keys[1], (N_PIPE, MB, D, TOK), 1.0, 6.0, ((0, 8), (2, 4)))
    gate_blocks = noise(arg_keys[2], (N_PIPE, N_TENSOR, COLS // 2, RCAP, BLK * BLK), (D // 4) ** -0.5, 0.1875, ((0, 8), (1, 4)))
    up_blocks = noise(arg_keys[3], (N_PIPE, N_TENSOR, COLS // 2, RCAP, BLK * BLK), (D // 4) ** -0.5, 0.1875, ((0, 8), (1, 4)))
    down_blocks = noise(arg_keys[4], (N_PIPE, N_TENSOR, COLS // 2, RCAP, BLK * BLK), (D // 4) ** -0.5, 0.1875, ((0, 8), (1, 4)))
    gate_rows = draw_gate_rows(jax.random.fold_in(arg_keys[7], 71), 0)
    down_rows = draw_down_rows(jax.random.fold_in(arg_keys[7], 71), 0)
    return {"x_saved": x_saved, "seed_grad": seed_grad, "gate_blocks": gate_blocks, "up_blocks": up_blocks, "down_blocks": down_blocks, "gate_rows": gate_rows, "down_rows": down_rows}


def column_products(tile_set, row_ids, source, pattern):
    columns, slot_depth = row_ids.shape
    filled = (row_ids >= 0).reshape(-1)
    picked = jnp.take(source, jnp.maximum(row_ids, 0).reshape(-1).astype(jnp.int32), axis=0)
    picked = jnp.where(filled[:, None, None], picked, jnp.zeros_like(picked))
    picked = picked.reshape(columns, slot_depth, BLK, source.shape[2])
    tile_grid = tile_set.reshape(columns, slot_depth, BLK, BLK)
    return jnp.einsum(pattern, tile_grid.astype(jnp.float32), picked.astype(jnp.float32))

def layer_branch(x_full, cot_full, gate_set, up_set, down_set, gate_ids, down_ids):
    tokens_now = x_full.shape[1]
    columns, slot_depth = gate_ids.shape
    x_blocks = x_full.reshape(RB, BLK, tokens_now)
    cot_blocks = cot_full.reshape(RB, BLK, tokens_now)
    gate_value = column_products(gate_set, gate_ids, x_blocks, 'crkj,crkt->cjt')
    up_value = column_products(up_set, gate_ids, x_blocks, 'crkj,crkt->cjt')
    d_hidden = column_products(down_set, down_ids, cot_blocks, 'crjk,crkt->cjt')
    sigmoid_gate = jax.nn.sigmoid(gate_value)
    d_gate = (d_hidden * up_value * sigmoid_gate * (1.0 + gate_value * (1.0 - sigmoid_gate))).astype(jnp.bfloat16)
    d_up = (d_hidden * gate_value * sigmoid_gate).astype(jnp.bfloat16)
    gate_grid = gate_set.reshape(columns, slot_depth, BLK, BLK).astype(jnp.float32)
    up_grid = up_set.reshape(columns, slot_depth, BLK, BLK).astype(jnp.float32)
    per_slot = jnp.einsum('crkj,cjt->crkt', gate_grid, d_gate.astype(jnp.float32))
    per_slot = per_slot + jnp.einsum('crkj,cjt->crkt', up_grid, d_up.astype(jnp.float32))
    segment_ids = jnp.where(gate_ids >= 0, gate_ids, RB).reshape(-1).astype(jnp.int32)
    summed = jax.ops.segment_sum(per_slot.reshape(columns * slot_depth, BLK, tokens_now), segment_ids, num_segments=RB + 1)
    return summed[:RB].reshape(RB * BLK, tokens_now)

def section_tiles(blocks, device):
    first_device = (2 * (device // 2)).astype(jnp.int32)
    pair_blocks = lax.dynamic_slice_in_dim(blocks, first_device, 2, 0)
    return jnp.concatenate([pair_blocks[0], pair_blocks[1]], axis=1)

def reference(x_saved, seed_grad, gate_blocks, up_blocks, down_blocks, gate_rows, down_rows):
    sections = N_PIPE // 2
    device_ids = jnp.arange(N_PIPE, dtype=jnp.int32)
    last_section = device_ids // 2 == sections - 1

    def device_grad(device_items):
        device, x_full, cot_full = device_items
        gate_all = section_tiles(gate_blocks, device)
        up_all = section_tiles(up_blocks, device)
        down_all = section_tiles(down_blocks, device)
        gate_all_ids = section_tiles(gate_rows, device)
        down_all_ids = section_tiles(down_rows, device)

        def shard_term(branch_total, shard_index):
            term = layer_branch(x_full, cot_full, gate_all[shard_index], up_all[shard_index], down_all[shard_index], gate_all_ids[shard_index], down_all_ids[shard_index])
            return (branch_total + term, None)
        branch_total, unused = lax.scan(shard_term, jnp.zeros((D, TOK), jnp.float32), jnp.arange(N_TENSOR, dtype=jnp.int32))
        return (cot_full.astype(jnp.float32) + branch_total).astype(jnp.bfloat16)
    results = []
    previous = None
    for micro_step in range(MB):
        if micro_step == 0:
            cotangent = seed_grad[:, 0]
        else:
            from_next = jnp.concatenate([previous[2:], jnp.zeros_like(previous[:2])], axis=0)
            cotangent = jnp.where(last_section[:, None, None], seed_grad[:, micro_step], from_next)
        previous = lax.map(device_grad, (device_ids, x_saved[:, micro_step], cotangent))
        results.append(previous)
    return jnp.stack(results, axis=1)
```

```python
import functools

import jax
import jax.numpy as jnp
from jax import lax
from jax.experimental import pallas as pl
from jax.experimental.pallas import tpu as pltpu
from jax.sharding import PartitionSpec as P

BLK = 64
BF16 = jnp.bfloat16
F32 = jnp.float32
MESH = pl.DeviceIdType.MESH


def kernel(
    n_pipe, n_tensor,
    gate_inv, down_inv, x_ref, seed_ref, pair_ref, down_ref, out_ref,
    xs, cs, w_nat, w_tr, w_down, gu, dh, dboth, sib_out, sib_in, red_out, red_in, own, arrived,
    ag_send, ag_recv, fw_send, fw_recv, sib_send_sem, sib_recv_sem, red_send_sem, red_recv_sem, z_send, z_recv,
):
    steps, rows, tok = x_ref.shape
    cols = w_nat.shape[1] // (2 * BLK)
    slots = pair_ref.shape[0] // cols
    half = n_tensor // 2
    chips = 2 * half
    p = lax.axis_index("pipe")
    t = lax.axis_index("tensor")
    ph, core, tc = p % 2, t % 2, t // 2
    base = p - ph
    has_next = p + 2 < n_pipe
    has_prev = p >= 2

    def at(dph, dtc, other=0):
        return (ph + dph) % 2, (tc + dtc) % half, (core + other) % 2

    def dev(dph, dtc):
        q, c, k = at(dph, dtc)
        return (base + q, c * 2 + k)

    sibling = (p, tc * 2 + (core + 1) % 2)
    peers = [(a, b) for b in range(half) for a in range(2) if a or b]
    order = [(a, b) for b in range(half) for a in range(2)]

    barrier = pltpu.get_barrier_semaphore()
    for a, b in peers:
        pl.semaphore_signal(barrier, inc=1, device_id=dev(a, b), device_id_type=MESH)
    pl.semaphore_signal(barrier, inc=1, device_id=sibling, device_id_type=MESH)

    @pl.when(has_next)
    def _():
        pl.semaphore_signal(barrier, inc=1, device_id=(p + 2, t), device_id_type=MESH)

    @pl.when(has_prev)
    def _():
        pl.semaphore_signal(barrier, inc=1, device_id=(p - 2, t), device_id_type=MESH)

    neighbours = chips + jnp.where(has_next, 1, 0) + jnp.where(has_prev, 1, 0)
    pl.semaphore_wait(barrier, neighbours)

    pending = []

    def slot(buf, q, c, k):
        return buf.at[
            pl.ds(pl.multiple_of((c * 2 + k) * rows, rows), rows),
            pl.ds(pl.multiple_of(q * tok, tok), tok),
        ]

    def remote(src, dst, s_sem, r_sem, device):
        return pltpu.make_async_remote_copy(
            src_ref=src, dst_ref=dst, send_sem=s_sem, recv_sem=r_sem, device_id=device, device_id_type=MESH
        )

    def gather_start(n, buf, src):
        mine = slot(buf, ph, tc, core)
        for a, b in peers:
            cp = remote(src, mine, ag_send.at[n, a * half + b], ag_recv.at[n, a * half + b], dev(a, b))
            cp.start()
            pending.append(cp)
        cp = remote(src, mine, fw_send.at[n, 0], fw_recv.at[n, 0], sibling)
        cp.start()
        pending.append(cp)
        buf[
            pl.ds(pl.multiple_of(t * rows, rows), rows), pl.ds(pl.multiple_of(ph * tok, tok), tok)
        ] = src[...]

    def gather_forward(n, buf):
        for a, b in peers:
            i = a * half + b
            got = slot(buf, *at(-a, -b))
            remote(got, got, ag_send.at[n, i], ag_recv.at[n, i], dev(a, b)).wait_recv()
            cp = remote(got, got, fw_send.at[n, i], fw_recv.at[n, i], sibling)
            cp.start()
            pending.append(cp)

    def gather_wait(n, buf):
        for a, b in order:
            i = a * half + b
            got = slot(buf, *at(-a, -b, 1))
            remote(got, got, fw_send.at[n, i], fw_recv.at[n, i], sibling).wait_recv()

    gather_start(0, xs.at[0], x_ref.at[0])
    gather_start(1, cs.at[0], seed_ref.at[0])

    lane_low = lax.broadcasted_iota(jnp.int32, (BLK, 2 * BLK), 1) < BLK
    zero = jnp.zeros((BLK, 2 * BLK), BF16)

    def build(lo, hi):
        def body(j, carry):
            at_row = pl.multiple_of(j * 2 * BLK, 2 * BLK)
            for c in range(cols):
                parts = []
                for e in range(2):
                    i = gate_inv[c, j * 2 + e]
                    tile = pair_ref[c * slots + jnp.maximum(i, 0)]
                    parts.append(jnp.where(i >= 0, tile, zero))
                block = jnp.concatenate(parts, axis=0)
                w_nat[pl.ds(at_row, 2 * BLK), c * 2 * BLK : (c + 1) * 2 * BLK] = block
                w_tr[c * 2 * BLK : (c + 1) * 2 * BLK, pl.ds(at_row, 2 * BLK)] = block.T
                i0 = down_inv[c, j * 2]
                i1 = down_inv[c, j * 2 + 1]
                t0 = jnp.where(i0 >= 0, down_ref[c * slots + jnp.maximum(i0, 0)], zero)
                t1 = jnp.where(i1 >= 0, down_ref[c * slots + jnp.maximum(i1, 0)], zero)
                w_down[c * BLK : (c + 1) * BLK, pl.ds(at_row, 2 * BLK)] = jnp.where(lane_low, t0, t1)
            return carry

        lax.fori_loop(lo, hi, body, 0)

    total = w_nat.shape[0] // (2 * BLK)
    build(0, total // 2)
    gather_forward(0, xs.at[0])
    for n in range(1, steps):
        gather_start(1 + n, xs.at[n], x_ref.at[n])
    build(total // 2, total)
    gather_forward(1, cs.at[0])

    def forward(n):
        gu[n] = jnp.zeros(gu.shape[1:], F32)

        def body(j, carry):
            r = pl.ds(pl.multiple_of(j * rows, rows), rows)
            gu[n] += jnp.dot(w_tr[:, r], xs[n, r, :], preferred_element_type=F32)
            return carry

        lax.fori_loop(0, n_tensor, body, 0)

    def hidden(n):
        dh[...] = jnp.zeros(dh.shape, F32)

        def body(j, carry):
            r = pl.ds(pl.multiple_of(j * rows, rows), rows)
            dh[...] += jnp.dot(w_down[:, r], cs[n, r, :], preferred_element_type=F32)
            return carry

        lax.fori_loop(0, n_tensor, body, 0)

        def act(c, carry):
            r2 = pl.multiple_of(c * 2 * BLK, 2 * BLK)
            g = gu[n, pl.ds(r2, BLK), :]
            u = gu[n, pl.ds(r2 + BLK, BLK), :]
            d = dh[pl.ds(pl.multiple_of(c * BLK, BLK), BLK), :]
            s = jax.nn.sigmoid(g)
            dboth[pl.ds(r2, BLK), :] = (d * u * s * (1.0 + g * (1.0 - s))).astype(BF16)
            dboth[pl.ds(r2 + BLK, BLK), :] = (d * g * s).astype(BF16)
            return carry

        lax.fori_loop(0, cols, act, 0)

    def branch(c, k):
        r = pl.ds(pl.multiple_of((c * 2 + k) * rows, rows), rows)
        return jnp.dot(w_nat[r, :], dboth[...], preferred_element_type=F32)

    def reduce_start(n):
        for b in list(range(1, half)) + [0]:
            _, c, k = at(0, b, 1)
            sib_out[n, b] = branch(c, k).astype(BF16)
            cp = remote(sib_out.at[n, b], sib_in.at[n, b], sib_send_sem.at[n, b], sib_recv_sem.at[n, b], sibling)
            cp.start()
            pending.append(cp)
        for b in list(range(1, half)) + [0]:
            _, c, k = at(0, b)
            part = branch(c, k)
            remote(
                sib_out.at[n, b], sib_in.at[n, b], sib_send_sem.at[n, b], sib_recv_sem.at[n, b], sibling
            ).wait_recv()
            part = part + sib_in[n, b].astype(F32)
            red_out[n, b] = part.astype(BF16)
            if b == 0:
                own[...] = part
            for a in range(2):
                if a or b:
                    q = (ph + a) % 2
                    cp = remote(
                        red_out.at[n, b, :, pl.ds(pl.multiple_of(q * tok, tok), tok)],
                        red_in.at[n, a * half + b],
                        red_send_sem.at[n, a * half + b],
                        red_recv_sem.at[n, a * half + b],
                        dev(a, b),
                    )
                    cp.start()
                    pending.append(cp)

    def reduce_finish(n, cot):
        acc = own[:, pl.ds(pl.multiple_of(ph * tok, tok), tok)]
        for a, b in peers:
            i = a * half + b
            remote(
                red_in.at[n, i], red_in.at[n, i], red_send_sem.at[n, i], red_recv_sem.at[n, i], dev(a, b)
            ).wait_recv()
            acc = acc + red_in[n, i].astype(F32)
        out_ref[n] = (cot.astype(F32) + acc).astype(BF16)

    gather_wait(0, xs.at[0])
    forward(0)
    gather_wait(1, cs.at[0])
    for n in range(steps):
        hidden(n)
        reduce_start(n)
        if n + 1 < steps:
            gather_forward(2 + n, xs.at[n + 1])
            gather_wait(2 + n, xs.at[n + 1])
            forward(n + 1)
        reduce_finish(n, seed_ref[0] if n == 0 else arrived[n - 1])
        if n + 1 < steps:
            hop = remote(out_ref.at[n], arrived.at[n], z_send.at[n], z_recv.at[n], (p - 2, t))

            @pl.when(has_prev)
            def _():
                hop.start()

            @pl.when(has_next)
            def _():
                hop.wait_recv()

            @pl.when(jnp.logical_not(has_next))
            def _():
                arrived[n] = seed_ref[n + 1]

            gather_start(steps + 1 + n, cs.at[n + 1], arrived.at[n])
            gather_forward(steps + 1 + n, cs.at[n + 1])
            gather_wait(steps + 1 + n, cs.at[n + 1])

            @pl.when(has_prev)
            def _():
                hop.wait_send()

    for cp in pending:
        cp.wait_send()


def per_device(n_pipe, n_tensor, x_saved, seed_grad, gate_blocks, up_blocks, down_blocks, gate_rows, down_rows):
    _, steps, rows, tok = x_saved.shape
    cols, slots = gate_rows.shape[2:]
    width = rows * n_tensor
    half = n_tensor // 2

    def inverse(ids):
        hit = ids[0, 0][:, :, None] == jnp.arange(width // BLK, dtype=jnp.int32)
        return jnp.max(jnp.where(hit, jnp.arange(slots, dtype=jnp.int32)[None, :, None], -1), axis=1)

    shape = (cols * slots, BLK, BLK)
    pair = jnp.concatenate([gate_blocks.reshape(shape), up_blocks.reshape(shape)], axis=2)
    down = down_blocks.reshape(shape)
    down = jnp.concatenate([down, down], axis=2)
    hid = cols * BLK
    gathers = 2 * steps
    dma = pltpu.SemaphoreType.DMA
    out = pl.pallas_call(
        functools.partial(kernel, n_pipe, n_tensor),
        out_shape=jax.ShapeDtypeStruct((steps, rows, tok), BF16),
        in_specs=[pl.BlockSpec(memory_space=pltpu.SMEM)] * 2 + [pl.BlockSpec(memory_space=pltpu.VMEM)] * 4,
        out_specs=pl.BlockSpec(memory_space=pltpu.VMEM),
        scratch_shapes=[
            pltpu.VMEM((steps, width, 2 * tok), BF16),
            pltpu.VMEM((steps, width, 2 * tok), BF16),
            pltpu.VMEM((width, 2 * hid), BF16),
            pltpu.VMEM((2 * hid, width), BF16),
            pltpu.VMEM((hid, width), BF16),
            pltpu.VMEM((steps, 2 * hid, 2 * tok), F32),
            pltpu.VMEM((hid, 2 * tok), F32),
            pltpu.VMEM((2 * hid, 2 * tok), BF16),
            pltpu.VMEM((steps, half, rows, 2 * tok), BF16),
            pltpu.VMEM((steps, half, rows, 2 * tok), BF16),
            pltpu.VMEM((steps, half, rows, 2 * tok), BF16),
            pltpu.VMEM((steps, n_tensor, rows, tok), BF16),
            pltpu.VMEM((rows, 2 * tok), F32),
            pltpu.VMEM((steps - 1, rows, tok), BF16),
            dma((gathers, n_tensor)),
            dma((gathers, n_tensor)),
            dma((gathers, n_tensor)),
            dma((gathers, n_tensor)),
            dma((steps, half)),
            dma((steps, half)),
            dma((steps, n_tensor)),
            dma((steps, n_tensor)),
            dma((steps,)),
            dma((steps,)),
        ],
        compiler_params=pltpu.CompilerParams(
            collective_id=0, has_side_effects=True, vmem_limit_bytes=58 * 1024 * 1024
        ),
    )(inverse(gate_rows), inverse(down_rows), x_saved[0], seed_grad[0], pair, down)
    return out[None]


def solution(mesh):
    return jax.shard_map(
        functools.partial(per_device, mesh.shape["pipe"], mesh.shape["tensor"]),
        mesh=mesh,
        in_specs=(
            P("pipe", None, "tensor", None),
            P("pipe", None, "tensor", None),
            P("pipe", "tensor", None, None, None),
            P("pipe", "tensor", None, None, None),
            P("pipe", "tensor", None, None, None),
            P("pipe", "tensor", None, None),
            P("pipe", "tensor", None, None),
        ),
        out_specs=P("pipe", None, "tensor", None),
        check_vma=False,
    )
```

```python
import functools

import jax
import jax.numpy as jnp
from jax import lax
from jax.experimental import pallas as pl
from jax.experimental.pallas import tpu as pltpu
from jax.sharding import PartitionSpec as P

BLK = 64
BF16 = jnp.bfloat16
F32 = jnp.float32
MESH = pl.DeviceIdType.MESH


def kernel(
    n_pipe, n_tensor,
    gate_inv, down_inv, x_ref, seed_ref, pair_ref, down_ref, out_ref,
    xs, cs, w_nat, w_tr, w_down, gu, dh, dboth, sib_out, sib_in, red_out, red_in, own, arrived,
    ag_send, ag_recv, fw_send, fw_recv, sib_send_sem, sib_recv_sem, red_send_sem, red_recv_sem, z_send, z_recv,
):
    steps, rows, tok = x_ref.shape
    cols = w_nat.shape[1] // (2 * BLK)
    slots = pair_ref.shape[0] // cols
    half = n_tensor // 2
    chips = 2 * half
    p = lax.axis_index("pipe")
    t = lax.axis_index("tensor")
    ph, core, tc = p % 2, t % 2, t // 2
    base = p - ph
    has_next = p + 2 < n_pipe
    has_prev = p >= 2

    def at(dph, dtc, other=0):
        return (ph + dph) % 2, (tc + dtc) % half, (core + other) % 2

    def dev(dph, dtc):
        q, c, k = at(dph, dtc)
        return (base + q, c * 2 + k)

    sibling = (p, tc * 2 + (core + 1) % 2)
    peers = [(a, b) for b in range(half) for a in range(2) if a or b]
    order = [(a, b) for b in range(half) for a in range(2)]

    barrier = pltpu.get_barrier_semaphore()
    for a, b in peers:
        pl.semaphore_signal(barrier, inc=1, device_id=dev(a, b), device_id_type=MESH)
    pl.semaphore_signal(barrier, inc=1, device_id=sibling, device_id_type=MESH)

    @pl.when(has_next)
    def _():
        pl.semaphore_signal(barrier, inc=1, device_id=(p + 2, t), device_id_type=MESH)

    @pl.when(has_prev)
    def _():
        pl.semaphore_signal(barrier, inc=1, device_id=(p - 2, t), device_id_type=MESH)

    neighbours = chips + jnp.where(has_next, 1, 0) + jnp.where(has_prev, 1, 0)
    pl.semaphore_wait(barrier, neighbours)

    pending = []

    def slot(buf, q, c, k):
        return buf.at[
            pl.ds(pl.multiple_of((c * 2 + k) * rows, rows), rows),
            pl.ds(pl.multiple_of(q * tok, tok), tok),
        ]

    def remote(src, dst, s_sem, r_sem, device):
        return pltpu.make_async_remote_copy(
            src_ref=src, dst_ref=dst, send_sem=s_sem, recv_sem=r_sem, device_id=device, device_id_type=MESH
        )

    def gather_start(n, buf, src):
        mine = slot(buf, ph, tc, core)
        for a, b in peers:
            cp = remote(src, mine, ag_send.at[n, a * half + b], ag_recv.at[n, a * half + b], dev(a, b))
            cp.start()
            pending.append(cp)
        cp = remote(src, mine, fw_send.at[n, 0], fw_recv.at[n, 0], sibling)
        cp.start()
        pending.append(cp)
        buf[
            pl.ds(pl.multiple_of(t * rows, rows), rows), pl.ds(pl.multiple_of(ph * tok, tok), tok)
        ] = src[...]

    def gather_forward(n, buf):
        for a, b in peers:
            i = a * half + b
            got = slot(buf, *at(-a, -b))
            remote(got, got, ag_send.at[n, i], ag_recv.at[n, i], dev(a, b)).wait_recv()
            cp = remote(got, got, fw_send.at[n, i], fw_recv.at[n, i], sibling)
            cp.start()
            pending.append(cp)

    def gather_wait(n, buf):
        for a, b in order:
            i = a * half + b
            got = slot(buf, *at(-a, -b, 1))
            remote(got, got, fw_send.at[n, i], fw_recv.at[n, i], sibling).wait_recv()

    gather_start(0, xs.at[0], x_ref.at[0])
    gather_start(1, cs.at[0], seed_ref.at[0])

    lane_low = lax.broadcasted_iota(jnp.int32, (BLK, 2 * BLK), 1) < BLK
    zero = jnp.zeros((BLK, 2 * BLK), BF16)

    def build(lo, hi):
        def body(j, carry):
            at_row = pl.multiple_of(j * 2 * BLK, 2 * BLK)
            for c in range(cols):
                parts = []
                for e in range(2):
                    i = gate_inv[c, j * 2 + e]
                    tile = pair_ref[c * slots + jnp.maximum(i, 0)]
                    parts.append(jnp.where(i >= 0, tile, zero))
                block = jnp.concatenate(parts, axis=0)
                w_nat[pl.ds(at_row, 2 * BLK), c * 2 * BLK : (c + 1) * 2 * BLK] = block
                w_tr[c * 2 * BLK : (c + 1) * 2 * BLK, pl.ds(at_row, 2 * BLK)] = block.T
                i0 = down_inv[c, j * 2]
                i1 = down_inv[c, j * 2 + 1]
                t0 = jnp.where(i0 >= 0, down_ref[c * slots + jnp.maximum(i0, 0)], zero)
                t1 = jnp.where(i1 >= 0, down_ref[c * slots + jnp.maximum(i1, 0)], zero)
                w_down[c * BLK : (c + 1) * BLK, pl.ds(at_row, 2 * BLK)] = jnp.where(lane_low, t0, t1)
            return carry

        lax.fori_loop(lo, hi, body, 0)

    total = w_nat.shape[0] // (2 * BLK)
    build(0, total // 2)
    gather_forward(0, xs.at[0])
    build(total // 2, total)
    gather_forward(1, cs.at[0])
    for n in range(1, steps):
        gather_start(1 + n, xs.at[n], x_ref.at[n])

    def forward(n):
        gu[n] = jnp.zeros(gu.shape[1:], F32)

        def body(j, carry):
            r = pl.ds(pl.multiple_of(j * rows, rows), rows)
            gu[n] += jnp.dot(w_tr[:, r], xs[n, r, :], preferred_element_type=F32)
            return carry

        lax.fori_loop(0, n_tensor, body, 0)

    def hidden(n):
        dh[...] = jnp.zeros(dh.shape, F32)

        def body(j, carry):
            r = pl.ds(pl.multiple_of(j * rows, rows), rows)
            dh[...] += jnp.dot(w_down[:, r], cs[n, r, :], preferred_element_type=F32)
            return carry

        lax.fori_loop(0, n_tensor, body, 0)

        def act(c, carry):
            r2 = pl.multiple_of(c * 2 * BLK, 2 * BLK)
            g = gu[n, pl.ds(r2, BLK), :]
            u = gu[n, pl.ds(r2 + BLK, BLK), :]
            d = dh[pl.ds(pl.multiple_of(c * BLK, BLK), BLK), :]
            s = jax.nn.sigmoid(g)
            dboth[pl.ds(r2, BLK), :] = (d * u * s * (1.0 + g * (1.0 - s))).astype(BF16)
            dboth[pl.ds(r2 + BLK, BLK), :] = (d * g * s).astype(BF16)
            return carry

        lax.fori_loop(0, cols, act, 0)

    def branch(c, k):
        r = pl.ds(pl.multiple_of((c * 2 + k) * rows, rows), rows)
        return jnp.dot(w_nat[r, :], dboth[...], preferred_element_type=F32)

    def reduce_start(n):
        for b in list(range(1, half)) + [0]:
            _, c, k = at(0, b, 1)
            sib_out[n, b] = branch(c, k).astype(BF16)
            cp = remote(sib_out.at[n, b], sib_in.at[n, b], sib_send_sem.at[n, b], sib_recv_sem.at[n, b], sibling)
            cp.start()
            pending.append(cp)
        for b in list(range(1, half)) + [0]:
            _, c, k = at(0, b)
            part = branch(c, k)
            remote(
                sib_out.at[n, b], sib_in.at[n, b], sib_send_sem.at[n, b], sib_recv_sem.at[n, b], sibling
            ).wait_recv()
            part = part + sib_in[n, b].astype(F32)
            red_out[n, b] = part.astype(BF16)
            if b == 0:
                own[...] = part
            for a in range(2):
                if a or b:
                    q = (ph + a) % 2
                    cp = remote(
                        red_out.at[n, b, :, pl.ds(pl.multiple_of(q * tok, tok), tok)],
                        red_in.at[n, a * half + b],
                        red_send_sem.at[n, a * half + b],
                        red_recv_sem.at[n, a * half + b],
                        dev(a, b),
                    )
                    cp.start()
                    pending.append(cp)

    def reduce_finish(n, cot):
        acc = own[:, pl.ds(pl.multiple_of(ph * tok, tok), tok)]
        for a, b in peers:
            i = a * half + b
            remote(
                red_in.at[n, i], red_in.at[n, i], red_send_sem.at[n, i], red_recv_sem.at[n, i], dev(a, b)
            ).wait_recv()
            acc = acc + red_in[n, i].astype(F32)
        out_ref[n] = (cot.astype(F32) + acc).astype(BF16)

    gather_wait(0, xs.at[0])
    forward(0)
    gather_wait(1, cs.at[0])
    for n in range(steps):
        hidden(n)
        reduce_start(n)
        if n + 1 < steps:
            gather_forward(2 + n, xs.at[n + 1])
            gather_wait(2 + n, xs.at[n + 1])
            forward(n + 1)
        reduce_finish(n, seed_ref[0] if n == 0 else arrived[n - 1])
        if n + 1 < steps:
            hop = remote(out_ref.at[n], arrived.at[n], z_send.at[n], z_recv.at[n], (p - 2, t))

            @pl.when(has_prev)
            def _():
                hop.start()

            @pl.when(has_next)
            def _():
                hop.wait_recv()

            @pl.when(jnp.logical_not(has_next))
            def _():
                arrived[n] = seed_ref[n + 1]

            gather_start(steps + 1 + n, cs.at[n + 1], arrived.at[n])
            gather_forward(steps + 1 + n, cs.at[n + 1])
            gather_wait(steps + 1 + n, cs.at[n + 1])

            @pl.when(has_prev)
            def _():
                hop.wait_send()

    for cp in pending:
        cp.wait_send()


def untangle(gate_ref, up_ref, down_ref, pair_ref, twin_ref, a_ref, b_ref):
    slots = gate_ref.shape[1]
    deep = BLK // 2
    low = lax.broadcasted_iota(jnp.int32, (deep, 2 * BLK), 1) < BLK

    def spread(src, dst):
        for k in range(deep):
            piece = src[0, :, k * 2 * BLK : (k + 1) * 2 * BLK].astype(F32)
            dst[pl.ds(k, slots, stride=deep), :] = piece

    def weave(left, right, out, tmp):
        def body(r, carry):
            rows = pl.ds(pl.multiple_of(r * deep, deep), deep)
            a = left[rows, :]
            b = right[rows, :]
            even = jnp.where(low, a, pltpu.roll(b, BLK, 1))
            odd = jnp.where(low, pltpu.roll(a, BLK, 1), b)
            tmp[pl.ds(0, deep, stride=2), :] = even
            tmp[pl.ds(1, deep, stride=2), :] = odd
            out[r] = tmp[...].astype(BF16)
            return carry

        lax.fori_loop(0, slots, body, 0, unroll=4)

    def run(tmp):
        spread(gate_ref, a_ref)
        spread(up_ref, b_ref)
        weave(a_ref, b_ref, pair_ref, tmp)
        spread(down_ref, a_ref)
        weave(a_ref, a_ref, twin_ref, tmp)

    pl.run_scoped(run, pltpu.VMEM((BLK, 2 * BLK), F32))


def tiles_of(gate_blocks, up_blocks, down_blocks):
    cols, slots, flat = gate_blocks.shape
    tile = jax.ShapeDtypeStruct((cols * slots, BLK, 2 * BLK), BF16)
    room = pltpu.VMEM(((slots + 7) // 8 * 8 * (BLK // 2) + BLK, 2 * BLK), F32)
    return pl.pallas_call(
        untangle,
        grid=(cols,),
        in_specs=[pl.BlockSpec((1, slots, flat), lambda c: (c, 0, 0))] * 3,
        out_specs=[pl.BlockSpec((slots, BLK, 2 * BLK), lambda c: (c, 0, 0))] * 2,
        out_shape=[tile, tile],
        scratch_shapes=[room, room],
    )(gate_blocks, up_blocks, down_blocks)


def per_device(n_pipe, n_tensor, x_saved, seed_grad, gate_blocks, up_blocks, down_blocks, gate_rows, down_rows):
    _, steps, rows, tok = x_saved.shape
    cols, slots = gate_rows.shape[2:]
    width = rows * n_tensor
    half = n_tensor // 2

    def inverse(ids):
        hit = ids[0, 0][:, :, None] == jnp.arange(width // BLK, dtype=jnp.int32)
        return jnp.max(jnp.where(hit, jnp.arange(slots, dtype=jnp.int32)[None, :, None], -1), axis=1)

    pair, down = tiles_of(gate_blocks[0, 0], up_blocks[0, 0], down_blocks[0, 0])
    hid = cols * BLK
    gathers = 2 * steps
    dma = pltpu.SemaphoreType.DMA
    out = pl.pallas_call(
        functools.partial(kernel, n_pipe, n_tensor),
        out_shape=jax.ShapeDtypeStruct((steps, rows, tok), BF16),
        in_specs=[pl.BlockSpec(memory_space=pltpu.SMEM)] * 2 + [pl.BlockSpec(memory_space=pltpu.VMEM)] * 4,
        out_specs=pl.BlockSpec(memory_space=pltpu.VMEM),
        scratch_shapes=[
            pltpu.VMEM((steps, width, 2 * tok), BF16),
            pltpu.VMEM((steps, width, 2 * tok), BF16),
            pltpu.VMEM((width, 2 * hid), BF16),
            pltpu.VMEM((2 * hid, width), BF16),
            pltpu.VMEM((hid, width), BF16),
            pltpu.VMEM((steps, 2 * hid, 2 * tok), F32),
            pltpu.VMEM((hid, 2 * tok), F32),
            pltpu.VMEM((2 * hid, 2 * tok), BF16),
            pltpu.VMEM((steps, half, rows, 2 * tok), BF16),
            pltpu.VMEM((steps, half, rows, 2 * tok), BF16),
            pltpu.VMEM((steps, half, rows, 2 * tok), BF16),
            pltpu.VMEM((steps, n_tensor, rows, tok), BF16),
            pltpu.VMEM((rows, 2 * tok), F32),
            pltpu.VMEM((steps - 1, rows, tok), BF16),
            dma((gathers, n_tensor)),
            dma((gathers, n_tensor)),
            dma((gathers, n_tensor)),
            dma((gathers, n_tensor)),
            dma((steps, half)),
            dma((steps, half)),
            dma((steps, n_tensor)),
            dma((steps, n_tensor)),
            dma((steps,)),
            dma((steps,)),
        ],
        compiler_params=pltpu.CompilerParams(
            collective_id=0, has_side_effects=True, vmem_limit_bytes=58 * 1024 * 1024
        ),
    )(inverse(gate_rows), inverse(down_rows), x_saved[0], seed_grad[0], pair, down)
    return out[None]


def solution(mesh):
    return jax.shard_map(
        functools.partial(per_device, mesh.shape["pipe"], mesh.shape["tensor"]),
        mesh=mesh,
        in_specs=(
            P("pipe", None, "tensor", None),
            P("pipe", None, "tensor", None),
            P("pipe", "tensor", None, None, None),
            P("pipe", "tensor", None, None, None),
            P("pipe", "tensor", None, None, None),
            P("pipe", "tensor", None, None),
            P("pipe", "tensor", None, None),
        ),
        out_specs=P("pipe", None, "tensor", None),
        check_vma=False,
    )
```
